128 devices in a mesh: term: 8 (over y, core), doc: 16 (over x, z).
Axes of the slice: x: 4, y: 4, z: 4, core: 2. Of those that a mesh axis runs over, the one named last changes fastest.
Arguments:
- doc_tiles: bfloat16 [8, 8192, 128, 128], P('term', 'doc'), may hold values from 0.049804688 to 3
- tile_rows: int32 [8, 8192], P('term', 'doc'), may hold values from 0 to 31
- tile_cols: int32 [8, 8192], P('term', 'doc'), may hold values from 0 to 511, as said below
- tile_count: int32 [8, 16], P('term', 'doc'), may hold values from 170 to 512, as said below
- factor_h: bfloat16 [128, 65536], P(None, ('term', 'doc')), may hold values from 0.049804688 to 1
- factor_w: float32 [32768, 128], P(('term', 'doc')), as said below
Outputs:
- new_w: float32 [32768, 128], P(('term', 'doc'))
The draws below stay inside these ranges and needn't reach their ends.
Inputs may be any that keep to these rules, and one draw needn't show every extreme that they name: Device (i, j) uses only the first tile_count[i, j] entries of its list of 512; some device's count is exactly 512. `tile_rows`: coordinates may repeat within a stripe; repeated tiles add. `tile_cols`: device (i, j)'s tiles belong to document shard j: every column block c in its list has (c // 4) % 16 == j, that is, c lies in the document columns that factor_h keeps on the devices (0, j), (1, j), ..., (7, j). `factor_w`: positive entries.
All inputs are finite; a program needn't handle non-finite values.
Results may differ from the reference program's by a relative error of at most 0.0003.
Values may be sent and summed in bfloat16 or wider, within the bound.
No kernel may reach another device: no remote copies, remote signals or barrier semaphores. Data moves between devices by JAX's collectives and lax.ppermute only.
A program may use at most 192 MiB of HBM per device.

```python
import math
import jax
import jax.numpy as jnp
import numpy as np
from jax import lax

K = 128
TB = 128
ND2 = 512
BLK = 512
RB = 32
M = 32768
N = 65536
N_TERM = 8
N_DOC = 16


def draw_tile_cols(key, part):
    key = jax.random.fold_in(key, 7)
    per_shard = ND2 // TB
    per_doc = N_TERM * per_shard
    local = jax.random.randint(key, (N_TERM, N_DOC * BLK), 0, per_doc)
    position = jnp.arange(N_TERM * N_DOC * BLK, dtype=jnp.int32).reshape(N_TERM, N_DOC * BLK)
    local = jnp.where(position == 0, 0, local)
    local = jnp.where(position == N_TERM * N_DOC * BLK - 1, per_doc - 1, local)
    doc_index = position % (N_DOC * BLK) // BLK
    term_part = local // per_shard
    within = local % per_shard
    cols = (term_part * N_DOC + doc_index) * per_shard + within
    return cols.astype(jnp.int32)


def draw_tile_count(key, part):
    key = jax.random.fold_in(key, 11)
    first, second = jax.random.split(key)
    counts = jax.random.randint(first, (N_TERM * N_DOC,), max(1, BLK // 3), BLK + 1)
    spot = jax.random.randint(second, (), 0, N_TERM * N_DOC)
    counts = jnp.where(jnp.arange(N_TERM * N_DOC) == spot, BLK, counts)
    return counts.reshape(N_TERM, N_DOC).astype(jnp.int32)


def draw_factor_w(key, part):
    key = jax.random.fold_in(key, 5)
    unit = jax.random.uniform(key, (M, K), jnp.float32)
    values = jnp.exp(jnp.log(0.001) + unit * jnp.log(100.0))
    return values.astype(jnp.float32)


def plant(result, rng, least, high):
    place = [jax.random.randint(jax.random.fold_in(rng, axis), (), 0, length) for axis, length in enumerate(result.shape)]
    main_axis = result.shape.index(max(result.shape))
    neighbour = place[:main_axis] + [(place[main_axis] + 1) % result.shape[main_axis]] + place[main_axis + 1:]
    return result.at[tuple(place)].set(least).at[tuple(neighbour)].set(high)


def block_levels(stream_key, dims, cuts, smallest, top_value):
    def one(axis_at, parts):
        steps = jax.random.uniform(jax.random.fold_in(jax.random.fold_in(stream_key, 6), axis_at), (parts,), jnp.float32, smallest / len(cuts), top_value / len(cuts))
        return jnp.repeat(jnp.exp(steps), dims[axis_at] // parts).reshape((-1,) + (1,) * (len(dims) - axis_at - 1))

    gain = one(*cuts[0])
    for cut in cuts[1:]:
        gain = gain * one(*cut)
    return gain


def cumulative_ranks(number_of, lean):
    loads = [(1 << 20) // math.isqrt(grade ** lean) + 1 for grade in range(1, number_of + 1)]
    width = 1 + sum(loads) // (1 << 30)
    return np.cumsum(np.array([max(1, weight // width) for weight in loads]))


def ranked(stream_key, dims, number_of, slope):
    table = cumulative_ranks(number_of, slope)
    lot = jax.random.randint(jax.random.fold_in(stream_key, 1), dims, 0, int(table[number_of - 1]))
    standing = jnp.searchsorted(jnp.asarray(table, jnp.int32), lot, side="right")
    return jax.random.permutation(jax.random.fold_in(stream_key, 2), number_of)[standing].astype(jnp.int32)


def setup_inputs(seed: int = 0) -> dict:
    key_list = jax.random.split(jax.random.key(seed), 7)
    doc_tiles = jnp.clip(jnp.exp(math.log(3.0) - 4.0982585 * jax.random.uniform(key_list[0], (N_TERM, N_DOC * BLK, TB, TB), jnp.float32) ** block_levels(key_list[0], (N_TERM, N_DOC * BLK, TB, TB), ((0, 8), (1, 16)), -0.2, 0.2)), 0.049804688, 3.0).astype(jnp.bfloat16)
    tile_rows = plant(ranked(key_list[1], (N_TERM, N_DOC * BLK), RB, 2), jax.random.fold_in(key_list[1], 3), 0, RB - 1).astype(jnp.int32)
    tile_cols = draw_tile_cols(jax.random.fold_in(key_list[6], 71), 0)
    tile_count = draw_tile_count(jax.random.fold_in(key_list[6], 71), 0)
    factor_h = jnp.clip(jnp.exp(math.log(1.0) - 2.9996462 * jax.random.uniform(key_list[4], (K, N), jnp.float32) ** block_levels(key_list[4], (K, N), ((1, 128),), -0.2, 0.2)), 0.049804688, 1.0).astype(jnp.bfloat16)
    factor_w = draw_factor_w(jax.random.fold_in(key_list[6], 71), 0)
    return dict(doc_tiles=doc_tiles, tile_rows=tile_rows, tile_cols=tile_cols, tile_count=tile_count, factor_h=factor_h, factor_w=factor_w)


def tile_products(block_list, row_list, col_list, live_count, h_blocks, row_blocks):
    picked = jnp.take(h_blocks, col_list, axis=1)
    products = jnp.einsum('btd,kbd->btk', block_list.astype(jnp.float32), picked.astype(jnp.float32))
    live_mask = (jnp.arange(block_list.shape[0], dtype=jnp.int32) < live_count).astype(jnp.float32)
    products = products * live_mask[:, None, None]
    return jax.ops.segment_sum(products, row_list, num_segments=row_blocks)

def hals_sweep(w_rows, cross_rows, gram):
    w_cols = w_rows.T
    a_cols = cross_rows.T

    def update(column, current):
        g_row = lax.dynamic_slice_in_dim(gram, column, 1, 0)
        projected = jnp.dot(g_row, current, precision=lax.Precision.HIGHEST)
        w_now = lax.dynamic_slice_in_dim(current, column, 1, 0)
        a_now = lax.dynamic_slice_in_dim(a_cols, column, 1, 0)
        g_diag = lax.dynamic_slice(gram, (column, column), (1, 1))
        fresh = jnp.maximum(w_now + (a_now - projected) / g_diag, 0.0)
        return lax.dynamic_update_slice_in_dim(current, fresh, column, 0)
    return lax.fori_loop(0, gram.shape[0], update, w_cols).T

def reference(doc_tiles, tile_rows, tile_cols, tile_count, factor_h, factor_w):
    h_blocks = factor_h.reshape(K, N // TB, TB)

    def stripe(operands):
        stripe_tiles, stripe_rows, stripe_cols, stripe_counts = operands

        def add_device(device, accum):
            start = jnp.asarray(device, jnp.int32) * BLK
            block_list = lax.dynamic_slice_in_dim(stripe_tiles, start, BLK, 0)
            row_list = lax.dynamic_slice_in_dim(stripe_rows, start, BLK, 0)
            col_list = lax.dynamic_slice_in_dim(stripe_cols, start, BLK, 0)
            live_count = lax.dynamic_index_in_dim(stripe_counts, jnp.asarray(device, jnp.int32), 0, keepdims=False)
            return accum + tile_products(block_list, row_list, col_list, live_count, h_blocks, RB)
        return lax.fori_loop(0, N_DOC, add_device, jnp.zeros((RB, TB, K), jnp.float32))
    cross = lax.map(stripe, (doc_tiles, tile_rows, tile_cols, tile_count)).reshape(M, K)
    gram = lax.dot_general(factor_h, factor_h, (((1,), (1,)), ((), ())), preferred_element_type=jnp.float32)
    updated = hals_sweep(factor_w, cross, gram)
    rms = jnp.sqrt(lax.optimization_barrier(jnp.sum(updated * updated, axis=0)) / M + 1e-06)
    return updated / rms
```

```python
import jax
import jax.numpy as jnp
from jax import lax
from jax.experimental import pallas as pl
from jax.experimental.pallas import tpu as pltpu
from jax.sharding import PartitionSpec as P

CHUNK = 32
UNROLL = 4
ANY = pl.ANY
VMEM = pltpu.VMEM
SMEM = pltpu.SMEM


def along_y(x, step):
    return lax.ppermute(x, "term", [(i, (i + 2 * step) % 8) for i in range(8)])


def other_core(x):
    return lax.ppermute(x, "term", [(i, i ^ 1) for i in range(8)])


def products_kernel(rows, blocks, count, near, far, tiles, out, held, h_all, sems):
    live = count[0]
    chunks = pl.cdiv(live, CHUNK)

    def fetch(c):
        part = pl.ds(c * CHUNK, CHUNK)
        return pltpu.make_async_copy(tiles.at[part], held.at[part], sems.at[c])

    @pl.loop(0, chunks)
    def _(c):
        fetch(c).start()

    out[...] = jnp.zeros_like(out)
    for s in range(4):
        for b in range(4):
            h_all[s * 4 + b] = near[s, b * 128 : (b + 1) * 128, :]
            h_all[16 + s * 4 + b] = far[s, b * 128 : (b + 1) * 128, :]
    h_all[32] = jnp.zeros((128, 128), jnp.bfloat16)

    @pl.loop(0, chunks)
    def _(c):
        fetch(c).wait()

        @pl.loop(0, CHUNK // UNROLL)
        def _(step):
            first = c * CHUNK + step * UNROLL
            found = []
            for u in range(UNROLL):
                e = first + u
                block = jnp.where(e < live, blocks[e], 32)
                found.append(jnp.dot(held[e], h_all[block], preferred_element_type=jnp.float32))
            for u in range(UNROLL):
                row = rows[first + u]
                out[row] += found[u]


def tile_products(rows, blocks, count, near, far, tiles):
    return pl.pallas_call(
        products_kernel,
        out_shape=jax.ShapeDtypeStruct((32, 128, 128), jnp.float32),
        in_specs=[pl.BlockSpec(memory_space=SMEM)] * 3
        + [pl.BlockSpec(memory_space=VMEM)] * 2
        + [pl.BlockSpec(memory_space=ANY)],
        out_specs=pl.BlockSpec(memory_space=VMEM),
        scratch_shapes=[
            VMEM((512, 128, 128), jnp.bfloat16),
            VMEM((33, 128, 128), jnp.bfloat16),
            pltpu.SemaphoreType.DMA((512 // CHUNK,)),
        ],
        compiler_params=pltpu.CompilerParams(vmem_limit_bytes=40 * 2**20),
    )(rows, blocks, count, near, far, tiles)


def sweep_kernel(parts, grams, w, fresh, squares):
    gram = grams[0]
    cross = parts[0]
    for j in range(1, 16):
        gram = gram + grams[j]
        cross = cross + parts[j]
    row_id = lax.broadcasted_iota(jnp.int32, (128, 128), 0)
    col_id = lax.broadcasted_iota(jnp.int32, (128, 128), 1)
    diagonal = jnp.sum(jnp.where(row_id == col_id, gram, 0.0), axis=1, keepdims=True)
    inverse = 1.0 / diagonal
    w_t = w[...].T
    rest = cross.T - jnp.dot(
        gram, w_t, precision=lax.Precision.HIGHEST, preferred_element_type=jnp.float32
    )
    estimate = w_t + rest * inverse
    scaled = jnp.where(col_id < row_id, gram * inverse, 0.0)
    groups = [estimate[8 * q : 8 * q + 8] for q in range(16)]
    for k in range(128):
        q, s = divmod(k, 8)
        change = jnp.maximum(groups[q][s : s + 1], 0.0) - w_t[k : k + 1]
        for later in range(q, 16):
            groups[later] = groups[later] - scaled[8 * later : 8 * later + 8, k : k + 1] * change
    updated = jnp.maximum(jnp.concatenate(groups, axis=0), 0.0).T
    fresh[...] = updated
    squares[...] = jnp.sum(updated * updated, axis=0, keepdims=True)


def sweep(parts, grams, w):
    return pl.pallas_call(
        sweep_kernel,
        out_shape=(
            jax.ShapeDtypeStruct((256, 128), jnp.float32),
            jax.ShapeDtypeStruct((1, 128), jnp.float32),
        ),
        in_specs=[pl.BlockSpec(memory_space=VMEM)] * 3,
        out_specs=[pl.BlockSpec(memory_space=VMEM)] * 2,
        compiler_params=pltpu.CompilerParams(vmem_limit_bytes=32 * 2**20),
    )(parts, grams, w)


def scale_kernel(total_rows, squares, updated, out):
    total = jnp.sum(squares[...], axis=0, keepdims=True)
    rms = jnp.sqrt(total / total_rows + 1e-06)
    out[...] = updated[...] / rms


def scale(squares, updated, total_rows):
    def kernel(*refs):
        scale_kernel(total_rows, *refs)

    return pl.pallas_call(
        kernel,
        out_shape=jax.ShapeDtypeStruct(updated.shape, jnp.float32),
    )(squares, updated)


def body(doc_tiles, tile_rows, tile_cols, tile_count, factor_h, factor_w):
    me = lax.axis_index("term")
    own = factor_h.T
    near = jnp.stack([own] + [along_y(own, s) for s in (1, 2, 3)])
    far = other_core(near)
    columns = tile_cols[0]
    owner = columns // 64
    blocks = (me // 2 - owner // 2) % 4 * 4 + columns % 4
    blocks = blocks + jnp.where(owner % 2 == me % 2, 0, 16)

    def self_gram(x):
        x = x.reshape(-1, 128)
        return lax.dot_general(x, x, (((0,), (0,)), ((), ())), preferred_element_type=jnp.float32)

    gram = self_gram(near) + self_gram(far)
    grams = lax.all_to_all(jnp.broadcast_to(gram, (16, 128, 128)), "doc", 0, 0)
    partial = tile_products(tile_rows[0], blocks, tile_count[0], near, far, doc_tiles[0])
    parts = lax.all_to_all(partial.reshape(16, 256, 128), "doc", 0, 0)
    updated, squares = sweep(parts, grams, factor_w)
    shared = lax.all_to_all(jnp.broadcast_to(squares, (128, 1, 128)), ("term", "doc"), 0, 0)
    return scale(shared.reshape(128, 128), updated, 32768)


def solution(mesh):
    in_specs = (
        P("term", "doc", None, None),
        P("term", "doc"),
        P("term", "doc"),
        P("term", "doc"),
        P(None, ("term", "doc")),
        P(("term", "doc"), None),
    )
    out_specs = P(("term", "doc"), None)
    return jax.shard_map(body, mesh=mesh, in_specs=in_specs, out_specs=out_specs, check_vma=False)
```

```python
import functools

import jax
import jax.numpy as jnp
from jax import lax
from jax.experimental import pallas as pl
from jax.experimental.pallas import tpu as pltpu
from jax.sharding import PartitionSpec as P

UNROLL = 16
ANY = pl.ANY
VMEM = pltpu.VMEM
SMEM = pltpu.SMEM


def along_y(x, step):
    return lax.ppermute(x, "term", [(i, (i + 2 * step) % 8) for i in range(8)])


def other_core(x):
    return lax.ppermute(x, "term", [(i, i ^ 1) for i in range(8)])


def along_x(x, step):
    return lax.ppermute(x, "doc", [(i, (i + 4 * step) % 16) for i in range(16)])


def along_z(x, step):
    return lax.ppermute(x, "doc", [(i, i // 4 * 4 + (i + step) % 4) for i in range(16)])


def resident(x):
    return pltpu.with_memory_space_constraint(x, VMEM)


def plan_kernel(rows, columns, count, plan):
    live = count[0, 0]
    c = columns[...]
    block = c // 64 * 4 + c % 4 + 1
    slot = lax.broadcasted_iota(jnp.int32, (1, 512), 1)
    row = jnp.where(slot < live, rows[...], 127)
    value = (slot + 1024 * block + 65536 * (row // 2)).astype(jnp.float32)
    lane = lax.broadcasted_iota(jnp.int32, (128, 128), 1)
    line = lax.broadcasted_iota(jnp.int32, (128, 128), 0)

    def down(x, g):
        return jnp.broadcast_to(x[:, 128 * g : 128 * g + 128], (128, 128)).T

    before = (lane < line).astype(jnp.bfloat16)
    row_f = row.astype(jnp.float32)
    members, ranks, total = [], [], jnp.zeros((1, 128), jnp.float32)
    for g in range(4):
        member = ((lane == down(row_f, g).astype(jnp.int32)) & (lane < 32)).astype(jnp.float32)
        rank = jnp.dot(before, member.astype(jnp.bfloat16), preferred_element_type=jnp.float32)
        ranks.append(rank + total)
        members.append(member)
        total = total + jnp.sum(member, axis=0, keepdims=True)
    groups = jnp.floor((total + 3.0) * 0.25)
    odd = lane % 2
    starts = 4.0 * jnp.dot(
        jnp.broadcast_to(groups, (8, 128)).astype(jnp.bfloat16),
        ((line < lane) & (line % 2 == odd)).astype(jnp.bfloat16),
        preferred_element_type=jnp.float32,
    )[:1]
    starts = starts + 640.0 * odd[:1].astype(jnp.float32)
    found = [jnp.zeros((1, 128), jnp.float32)] * 10
    for g in range(4):
        position = jnp.sum(members[g] * (ranks[g] + starts), axis=1, keepdims=True)
        alive = jnp.sum(members[g], axis=1, keepdims=True)
        position = jnp.where(alive > 0.0, position, -1.0).astype(jnp.int32)
        values = down(value, g)
        for t in range(10):
            hit = jnp.where(position == lane + 128 * t, values, 0.0)
            found[t] = found[t] + jnp.sum(hit, axis=0, keepdims=True)
    for t in range(10):
        plan[t : t + 1] = found[t].astype(jnp.int32)
    for half in range(2):
        mine = jnp.where(odd[:1] == half, groups, 0.0)
        quads = jnp.sum(mine, axis=1, keepdims=True).astype(jnp.int32)
        plan[10 + half : 11 + half] = jnp.broadcast_to(quads, (1, 128))
    plan[12:16] = jnp.zeros((4, 128), jnp.int32)


def make_plan(rows, columns, count):
    return pl.pallas_call(
        plan_kernel,
        out_shape=jax.ShapeDtypeStruct((16, 128), jnp.int32),
        in_specs=[pl.BlockSpec(memory_space=VMEM)] * 2 + [pl.BlockSpec(memory_space=SMEM)],
        out_specs=pl.BlockSpec(memory_space=VMEM),
        cost_estimate=pl.CostEstimate(flops=10**8, bytes_accessed=10**5, transcendentals=0),
        compiler_params=pltpu.CompilerParams(vmem_limit_bytes=8 * 2**20),
    )(rows, columns, count)


def products_kernel(half, plan_in, near, far, gram, tiles, *refs):
    outs, (sums, h_all, plan, plan_sem) = refs[:4], refs[4:]
    plan_copy = pltpu.make_async_copy(plan_in, plan, plan_sem)
    plan_copy.start()
    me, doc = lax.axis_index("term"), lax.axis_index("doc")
    my_x, my_z = doc // 4, lax.rem(doc, 4)
    sums[...] = jnp.zeros_like(sums)
    h_all[0] = jnp.zeros((128, 128), jnp.bfloat16)
    for s in range(4):
        for b in range(4):
            same = lax.rem(me + 8 - 2 * s, 8)
            other = same + 1 - 2 * lax.rem(me, 2)
            h_all[1 + same * 4 + b] = near[s, b * 128 : (b + 1) * 128, :]
            h_all[1 + other * 4 + b] = far[s, b * 128 : (b + 1) * 128, :]
    plan_copy.wait()

    @pl.loop(0, pl.cdiv(plan[10 + half, 0], UNROLL))
    def _(step):
        found, targets = [], []
        for u in range(UNROLL):
            first = (step * UNROLL + u) * 4
            left, right = [], []
            for i in range(4):
                entry = plan[5 * half + first // 128, first % 128 + i]
                left.append(tiles[entry & 1023])
                right.append(h_all[(entry >> 10) & 63])
                if i == 0:
                    to_x, to_z = entry >> 18, (entry >> 16) & 3
                    if half == 0:
                        targets.append(((to_x + 4 - my_x) & 3) * 4 + to_z)
                    else:
                        targets.append(((to_z + 4 - my_z) & 3) * 4 + to_x)
            found.append(
                jnp.dot(
                    jnp.concatenate(left, axis=1),
                    jnp.concatenate(right, axis=0),
                    preferred_element_type=jnp.float32,
                )
            )
        for u in range(UNROLL):
            sums[targets[u]] += found[u]

    for s in range(4):
        for b in range(4):
            outs[s][b * 128 : b * 128 + 128] = sums[4 * s + b]
        outs[s][512:576] = gram[64 * half : 64 * half + 64]


def tile_products(half, plan, near, far, gram, tiles):
    return pl.pallas_call(
        functools.partial(products_kernel, half),
        out_shape=[jax.ShapeDtypeStruct((576, 128), jnp.float32)] * 4,
        in_specs=[pl.BlockSpec(memory_space=ANY)] + [pl.BlockSpec(memory_space=VMEM)] * 4,
        out_specs=[pl.BlockSpec(memory_space=VMEM)] * 4,
        scratch_shapes=[
            VMEM((16, 128, 128), jnp.float32),
            VMEM((33, 128, 128), jnp.bfloat16),
            SMEM((16, 128), jnp.int32),
            pltpu.SemaphoreType.DMA,
        ],
        cost_estimate=pl.CostEstimate(flops=4 * 10**9, bytes_accessed=10**7, transcendentals=0),
        compiler_params=pltpu.CompilerParams(vmem_limit_bytes=8 * 2**20),
    )(plan, near, far, gram, resident(tiles))


def regroup_kernel(half, *refs):
    pieces, outs = refs[:4], refs[-4:]
    doc = lax.axis_index("doc")
    mine = lax.rem(doc, 4) if half == 0 else doc // 4
    for s in range(4):
        first = pl.multiple_of(((mine + s) & 3) * 128, 128)
        part = pl.ds(first, 128)
        outs[s][0:128] = (pieces[0][part] + pieces[1][part]) + (pieces[2][part] + pieces[3][part])
    gram = (pieces[0][512:576] + pieces[1][512:576]) + (pieces[2][512:576] + pieces[3][512:576])
    for s in range(4):
        outs[s][128:192] = gram


def regroup(half, pieces, after=()):
    return pl.pallas_call(
        functools.partial(regroup_kernel, half),
        out_shape=[jax.ShapeDtypeStruct((192, 128), jnp.float32)] * 4,
        in_specs=[pl.BlockSpec(memory_space=VMEM)] * 4
        + [pl.BlockSpec(memory_space=ANY)] * len(after),
        out_specs=[pl.BlockSpec(memory_space=VMEM)] * 4,
        compiler_params=pltpu.CompilerParams(vmem_limit_bytes=8 * 2**20),
    )(*pieces, *after)


def sweep_kernel(*refs):
    first, second, (w, fresh, squares) = refs[:4], refs[4:8], refs[8:]
    upper = (first[0][...] + first[1][...]) + (first[2][...] + first[3][...])
    lower = (second[0][...] + second[1][...]) + (second[2][...] + second[3][...])
    cross_t = jnp.concatenate([upper[:128].T, lower[:128].T], axis=1)
    gram = jnp.concatenate([upper[128:], lower[128:]], axis=0)
    row_id = lax.broadcasted_iota(jnp.int32, (128, 128), 0)
    col_id = lax.broadcasted_iota(jnp.int32, (128, 128), 1)
    diagonal = jnp.sum(jnp.where(row_id == col_id, gram, 0.0), axis=1, keepdims=True)
    inverse = 1.0 / diagonal
    w_t = w[...].T
    rest = cross_t - jnp.dot(
        gram, w_t, precision=lax.Precision.HIGHEST, preferred_element_type=jnp.float32
    )
    estimate = w_t + rest * inverse
    scaled = jnp.where(col_id < row_id, gram * inverse, 0.0)
    groups = [estimate[8 * q : 8 * q + 8] for q in range(16)]
    for k in range(128):
        q, s = divmod(k, 8)
        change = jnp.maximum(groups[q][s : s + 1], 0.0) - w_t[k : k + 1]
        for later in range(q, 16):
            groups[later] = groups[later] - scaled[8 * later : 8 * later + 8, k : k + 1] * change
    updated = jnp.maximum(jnp.concatenate(groups, axis=0), 0.0).T
    fresh[...] = updated
    squares[...] = jnp.broadcast_to(
        jnp.sum(updated * updated, axis=0, keepdims=True), (128, 128)
    )


def sweep(first, second, w):
    return pl.pallas_call(
        sweep_kernel,
        out_shape=(
            jax.ShapeDtypeStruct((256, 128), jnp.float32),
            jax.ShapeDtypeStruct((128, 128), jnp.float32),
        ),
        in_specs=[pl.BlockSpec(memory_space=VMEM)] * 9,
        out_specs=[pl.BlockSpec(memory_space=VMEM)] * 2,
        compiler_params=pltpu.CompilerParams(vmem_limit_bytes=16 * 2**20),
    )(*first, *second, w)


def scale_kernel(total_rows, squares, updated, out):
    total = jnp.sum(squares[...], axis=0, keepdims=True)
    rms = jnp.sqrt(total / total_rows + 1e-06)
    out[...] = updated[...] / rms


def scale(squares, updated, total_rows):
    return pl.pallas_call(
        functools.partial(scale_kernel, total_rows),
        out_shape=jax.ShapeDtypeStruct(updated.shape, jnp.float32),
    )(resident(squares), resident(updated))


def body(doc_tiles, tile_rows, tile_cols, tile_count, factor_h, factor_w):
    tiles = doc_tiles[0]
    own = factor_h.T
    shifted = [along_y(own, s) for s in (1, 2, 3)]
    plan = make_plan(tile_rows, tile_cols, tile_count)
    near, plan = lax.optimization_barrier((jnp.stack([own] + shifted), plan))
    far = other_core(near)

    def self_gram(x):
        x = x.reshape(-1, 128)
        return lax.dot_general(x, x, (((0,), (0,)), ((), ())), preferred_element_type=jnp.float32)

    gram = self_gram(near) + self_gram(far)
    even = tile_products(0, plan, near, far, gram, tiles)
    odd = tile_products(1, plan, near, far, gram, tiles)
    after = odd[0]
    even = [even[0]] + [along_x(even[s], s) for s in (1, 2, 3)]
    odd = [odd[0]] + [along_z(odd[s], s) for s in (1, 2, 3)]
    even = regroup(0, even, [after])
    even = [even[0]] + [along_z(even[s], s) for s in (1, 2, 3)]
    odd = regroup(1, odd)
    odd = [odd[0]] + [along_x(odd[s], s) for s in (1, 2, 3)]
    updated, squares = sweep(even, odd, factor_w)
    shared = lax.all_to_all(squares.reshape(128, 1, 128), ("term", "doc"), 0, 0)
    return scale(shared.reshape(128, 128), updated, 32768)


def solution(mesh):
    in_specs = (
        P("term", "doc", None, None),
        P("term", "doc"),
        P("term", "doc"),
        P("term", "doc"),
        P(None, ("term", "doc")),
        P(("term", "doc"), None),
    )
    out_specs = P(("term", "doc"), None)
    return jax.shard_map(body, mesh=mesh, in_specs=in_specs, out_specs=out_specs, check_vma=False)
```

```python
import functools

import jax
import jax.numpy as jnp
from jax import lax
from jax.experimental import pallas as pl
from jax.experimental.pallas import tpu as pltpu
from jax.sharding import PartitionSpec as P

UNROLL = 24
ANY = pl.ANY
VMEM = pltpu.VMEM
SMEM = pltpu.SMEM


def along_y(x, step):
    return lax.ppermute(x, "term", [(i, (i + 2 * step) % 8) for i in range(8)])


def other_core(x):
    return lax.ppermute(x, "term", [(i, i ^ 1) for i in range(8)])


def along_x(x, step):
    return lax.ppermute(x, "doc", [(i, (i + 4 * step) % 16) for i in range(16)])


def along_z(x, step):
    return lax.ppermute(x, "doc", [(i, i // 4 * 4 + (i + step) % 4) for i in range(16)])


def in_hbm(x):
    return pltpu.with_memory_space_constraint(x, pltpu.HBM)


def resident(x):
    return pltpu.with_memory_space_constraint(x, VMEM)


def plan_kernel(rows_in, columns_in, count, tiles, plan, rows, columns, sems):
    rows_copy = pltpu.make_async_copy(rows_in, rows, sems.at[0])
    columns_copy = pltpu.make_async_copy(columns_in, columns, sems.at[1])
    rows_copy.start()
    columns_copy.start()
    rows_copy.wait()
    columns_copy.wait()
    live = count[0, 0]
    c = columns[...]
    block = c // 64 * 4 + c % 4 + 1
    slot = lax.broadcasted_iota(jnp.int32, (1, 512), 1)
    row = jnp.where(slot < live, rows[...], 127)
    value = (slot + 1024 * block + 65536 * (row // 2)).astype(jnp.float32)
    lane = lax.broadcasted_iota(jnp.int32, (128, 128), 1)
    line = lax.broadcasted_iota(jnp.int32, (128, 128), 0)

    def down(x, g):
        return jnp.broadcast_to(x[:, 128 * g : 128 * g + 128], (128, 128)).T

    before = (lane < line).astype(jnp.bfloat16)
    row_f = row.astype(jnp.float32)
    members, ranks, total = [], [], jnp.zeros((1, 128), jnp.float32)
    for g in range(4):
        member = ((lane == down(row_f, g).astype(jnp.int32)) & (lane < 32)).astype(jnp.float32)
        rank = jnp.dot(before, member.astype(jnp.bfloat16), preferred_element_type=jnp.float32)
        ranks.append(rank + total)
        members.append(member)
        total = total + jnp.sum(member, axis=0, keepdims=True)
    groups = jnp.floor((total + 3.0) * 0.25)
    odd = lane % 2
    starts = 4.0 * jnp.dot(
        jnp.broadcast_to(groups, (8, 128)).astype(jnp.bfloat16),
        ((line < lane) & (line % 2 == odd)).astype(jnp.bfloat16),
        preferred_element_type=jnp.float32,
    )[:1]
    starts = starts + 640.0 * odd[:1].astype(jnp.float32)
    found = [jnp.zeros((1, 128), jnp.float32)] * 10
    for g in range(4):
        position = jnp.sum(members[g] * (ranks[g] + starts), axis=1, keepdims=True)
        alive = jnp.sum(members[g], axis=1, keepdims=True)
        position = jnp.where(alive > 0.0, position, -1.0).astype(jnp.int32)
        values = down(value, g)
        for t in range(10):
            hit = jnp.where(position == lane + 128 * t, values, 0.0)
            found[t] = found[t] + jnp.sum(hit, axis=0, keepdims=True)
    for t in range(10):
        plan[t : t + 1] = found[t].astype(jnp.int32)
    for half in range(2):
        mine = jnp.where(odd[:1] == half, groups, 0.0)
        quads = jnp.sum(mine, axis=1, keepdims=True).astype(jnp.int32)
        plan[10 + half : 11 + half] = jnp.broadcast_to(quads, (1, 128))
    plan[12:16] = jnp.zeros((4, 128), jnp.int32)


def make_plan(rows, columns, count, tiles):
    return pl.pallas_call(
        plan_kernel,
        out_shape=jax.ShapeDtypeStruct((16, 128), jnp.int32),
        in_specs=[pl.BlockSpec(memory_space=ANY)] * 2
        + [pl.BlockSpec(memory_space=SMEM), pl.BlockSpec(memory_space=VMEM)],
        out_specs=pl.BlockSpec(memory_space=VMEM),
        scratch_shapes=[
            VMEM((1, 512), jnp.int32),
            VMEM((1, 512), jnp.int32),
            pltpu.SemaphoreType.DMA((2,)),
        ],
        cost_estimate=pl.CostEstimate(flops=10**8, bytes_accessed=10**5, transcendentals=0),
        compiler_params=pltpu.CompilerParams(vmem_limit_bytes=8 * 2**20),
    )(in_hbm(rows), in_hbm(columns), count, resident(tiles))


def partial_gram(shards):
    total = None
    for s in range(4):
        x = shards[s]
        part = lax.dot_general(x, x, (((0,), (0,)), ((), ())), preferred_element_type=jnp.float32)
        total = part if total is None else total + part
    return total


def pack(shards):
    return pl.pallas_call(
        pack_only_kernel,
        out_shape=jax.ShapeDtypeStruct((4, 512, 128), jnp.bfloat16),
        in_specs=[pl.BlockSpec(memory_space=VMEM)] * 4,
        out_specs=pl.BlockSpec(memory_space=VMEM),
        compiler_params=pltpu.CompilerParams(vmem_limit_bytes=4 * 2**20),
    )(*shards)


def pack_only_kernel(own, first, second, third, near):
    for s, shard in enumerate((own, first, second, third)):
        near[s] = shard[...]


def gram_kernel(shards, gram):
    gram[...] = partial_gram(shards)


def gram_of(shards):
    return pl.pallas_call(
        gram_kernel,
        out_shape=jax.ShapeDtypeStruct((128, 128), jnp.float32),
        in_specs=[pl.BlockSpec(memory_space=VMEM)],
        out_specs=pl.BlockSpec(memory_space=VMEM),
        compiler_params=pltpu.CompilerParams(vmem_limit_bytes=4 * 2**20),
    )(shards)


def products_kernel(half, plan_in, near, far, gram, tiles, *refs):
    outs, (sums, h_all, plan, plan_sem) = refs[:4], refs[4:]
    plan_copy = pltpu.make_async_copy(plan_in, plan, plan_sem)
    plan_copy.start()
    me, doc = lax.axis_index("term"), lax.axis_index("doc")
    my_x, my_z = doc // 4, lax.rem(doc, 4)
    sums[...] = jnp.zeros_like(sums)
    h_all[0] = jnp.zeros((128, 128), jnp.bfloat16)
    for s in range(4):
        for b in range(4):
            same = lax.rem(me + 8 - 2 * s, 8)
            other = same + 1 - 2 * lax.rem(me, 2)
            h_all[1 + same * 4 + b] = near[s, b * 128 : (b + 1) * 128, :]
            h_all[1 + other * 4 + b] = far[s, b * 128 : (b + 1) * 128, :]
    if half == 0:
        whole_gram = gram[...] + partial_gram(far)
    plan_copy.wait()

    @pl.loop(0, pl.cdiv(plan[10 + half, 0], UNROLL))
    def _(step):
        found, targets = [], []
        for u in range(UNROLL):
            first = (step * UNROLL + u) * 4
            left, right = [], []
            for i in range(4):
                entry = plan[5 * half + first // 128, first % 128 + i]
                left.append(tiles[entry & 1023])
                right.append(h_all[(entry >> 10) & 63])
                if i == 0:
                    to_x, to_z = entry >> 18, (entry >> 16) & 3
                    if half == 0:
                        targets.append(((to_x + 4 - my_x) & 3) * 4 + to_z)
                    else:
                        targets.append(((to_z + 4 - my_z) & 3) * 4 + to_x)
            found.append(
                jnp.dot(
                    jnp.concatenate(left, axis=1),
                    jnp.concatenate(right, axis=0),
                    preferred_element_type=jnp.float32,
                )
            )
        for u in range(UNROLL):
            sums[targets[u]] += found[u]

    for s in range(4):
        for b in range(4):
            outs[s][b * 128 : b * 128 + 128] = sums[4 * s + b]
        if half == 0:
            outs[s][512:640] = whole_gram


def tile_products(half, plan, near, far, gram, tiles):
    return pl.pallas_call(
        functools.partial(products_kernel, half),
        out_shape=[jax.ShapeDtypeStruct((640 if half == 0 else 512, 128), jnp.float32)] * 4,
        in_specs=[pl.BlockSpec(memory_space=ANY)] + [pl.BlockSpec(memory_space=VMEM)] * 4,
        out_specs=[pl.BlockSpec(memory_space=VMEM)] * 4,
        scratch_shapes=[
            VMEM((16, 128, 128), jnp.float32),
            VMEM((33, 128, 128), jnp.bfloat16),
            SMEM((16, 128), jnp.int32),
            pltpu.SemaphoreType.DMA,
        ],
        cost_estimate=pl.CostEstimate(flops=10**9, bytes_accessed=10**7, transcendentals=0),
        compiler_params=pltpu.CompilerParams(vmem_limit_bytes=8 * 2**20),
    )(plan, near, far, gram, resident(tiles))


def regroup_kernel(half, *refs):
    pieces, outs = refs[:4], refs[-4:]
    doc = lax.axis_index("doc")
    mine = lax.rem(doc, 4) if half == 0 else doc // 4
    for s in range(4):
        first = pl.multiple_of(((mine + s) & 3) * 128, 128)
        part = pl.ds(first, 128)
        outs[s][0:128] = (pieces[0][part] + pieces[1][part]) + (pieces[2][part] + pieces[3][part])
    if half == 0:
        gram = (pieces[0][512:] + pieces[1][512:]) + (pieces[2][512:] + pieces[3][512:])
        for s in range(4):
            outs[s][128:256] = gram


def regroup(half, pieces, after=()):
    return pl.pallas_call(
        functools.partial(regroup_kernel, half),
        out_shape=[jax.ShapeDtypeStruct((256 if half == 0 else 128, 128), jnp.float32)] * 4,
        in_specs=[pl.BlockSpec(memory_space=VMEM)] * 4
        + [pl.BlockSpec(memory_space=ANY)] * len(after),
        out_specs=[pl.BlockSpec(memory_space=VMEM)] * 4,
        compiler_params=pltpu.CompilerParams(vmem_limit_bytes=8 * 2**20),
    )(*pieces, *after)


def sweep_kernel(*refs):
    first, second, (w, fresh, squares) = refs[:4], refs[4:8], refs[8:]
    upper = (first[0][...] + first[1][...]) + (first[2][...] + first[3][...])
    lower = (second[0][...] + second[1][...]) + (second[2][...] + second[3][...])
    cross_t = jnp.concatenate([upper[:128].T, lower.T], axis=1)
    gram = upper[128:]
    row_id = lax.broadcasted_iota(jnp.int32, (128, 128), 0)
    col_id = lax.broadcasted_iota(jnp.int32, (128, 128), 1)
    diagonal = jnp.sum(jnp.where(row_id == col_id, gram, 0.0), axis=1, keepdims=True)
    inverse = 1.0 / diagonal
    w_t = w[...].T
    rest = cross_t - jnp.dot(
        gram, w_t, precision=lax.Precision.HIGHEST, preferred_element_type=jnp.float32
    )
    estimate = w_t + rest * inverse
    scaled = jnp.where(col_id < row_id, gram * inverse, 0.0)
    groups = [estimate[8 * q : 8 * q + 8] for q in range(16)]
    for k in range(128):
        q, s = divmod(k, 8)
        change = jnp.maximum(groups[q][s : s + 1], 0.0) - w_t[k : k + 1]
        for later in range(q, 16):
            groups[later] = groups[later] - scaled[8 * later : 8 * later + 8, k : k + 1] * change
    updated = jnp.maximum(jnp.concatenate(groups, axis=0), 0.0).T
    fresh[...] = updated
    squares[...] = jnp.broadcast_to(
        jnp.sum(updated * updated, axis=0, keepdims=True), (128, 128)
    )


def sweep(first, second, w):
    return pl.pallas_call(
        sweep_kernel,
        out_shape=(
            jax.ShapeDtypeStruct((256, 128), jnp.float32),
            jax.ShapeDtypeStruct((128, 128), jnp.float32),
        ),
        in_specs=[pl.BlockSpec(memory_space=VMEM)] * 9,
        out_specs=[pl.BlockSpec(memory_space=VMEM)] * 2,
        compiler_params=pltpu.CompilerParams(vmem_limit_bytes=16 * 2**20),
    )(*first, *second, w)


def scale_kernel(total_rows, squares, updated, out):
    total = jnp.sum(squares[...], axis=0, keepdims=True)
    rms = jnp.sqrt(total / total_rows + 1e-06)
    out[...] = updated[...] / rms


def scale(squares, updated, total_rows):
    return pl.pallas_call(
        functools.partial(scale_kernel, total_rows),
        out_shape=jax.ShapeDtypeStruct(updated.shape, jnp.float32),
    )(resident(squares), resident(updated))


def body(doc_tiles, tile_rows, tile_cols, tile_count, factor_h, factor_w):
    tiles = doc_tiles[0]
    own = factor_h.T
    shifted = [along_y(own, s) for s in (1, 2, 3)]
    plan = make_plan(tile_rows, tile_cols, tile_count, tiles)
    near, plan = lax.optimization_barrier((pack([own] + shifted), plan))
    far = other_core(near)

    gram = gram_of(near)
    even = tile_products(0, plan, near, far, gram, tiles)
    odd = tile_products(1, plan, near, far, gram, tiles)
    after = odd[0]
    even = [even[0]] + [along_x(even[s], s) for s in (1, 2, 3)]
    odd = [odd[0]] + [along_z(odd[s], s) for s in (1, 2, 3)]
    even = regroup(0, even, [after])
    even = [even[0]] + [along_z(even[s], s) for s in (1, 2, 3)]
    odd = regroup(1, odd)
    odd = [odd[0]] + [along_x(odd[s], s) for s in (1, 2, 3)]
    updated, squares = sweep(even, odd, factor_w)
    shared = lax.all_to_all(squares.reshape(128, 1, 128), ("term", "doc"), 0, 0)
    return scale(shared.reshape(128, 128), updated, 32768)


def solution(mesh):
    in_specs = (
        P("term", "doc", None, None),
        P("term", "doc"),
        P("term", "doc"),
        P("term", "doc"),
        P(None, ("term", "doc")),
        P(("term", "doc"), None),
    )
    out_specs = P(("term", "doc"), None)
    return jax.shard_map(body, mesh=mesh, in_specs=in_specs, out_specs=out_specs, check_vma=False)
```

```python
import functools

import jax
import jax.numpy as jnp
from jax import lax
from jax.experimental import pallas as pl
from jax.experimental.pallas import tpu as pltpu
from jax.sharding import PartitionSpec as P

UNROLL = 24
ANY = pl.ANY
VMEM = pltpu.VMEM
SMEM = pltpu.SMEM


def along_y(x, step):
    return lax.ppermute(x, "term", [(i, (i + 2 * step) % 8) for i in range(8)])


def other_core(x):
    return lax.ppermute(x, "term", [(i, i ^ 1) for i in range(8)])


def along_x(x, step):
    return lax.ppermute(x, "doc", [(i, (i + 4 * step) % 16) for i in range(16)])


def along_z(x, step):
    return lax.ppermute(x, "doc", [(i, i // 4 * 4 + (i + step) % 4) for i in range(16)])


def in_hbm(x):
    return pltpu.with_memory_space_constraint(x, pltpu.HBM)


def resident(x):
    return pltpu.with_memory_space_constraint(x, VMEM)


def plan_kernel(rows_in, columns_in, count, tiles, plan, rows, columns, sems):
    rows_copy = pltpu.make_async_copy(rows_in, rows, sems.at[0])
    columns_copy = pltpu.make_async_copy(columns_in, columns, sems.at[1])
    rows_copy.start()
    columns_copy.start()
    rows_copy.wait()
    columns_copy.wait()
    live = count[0, 0]
    c = columns[...]
    block = c // 64 * 4 + c % 4 + 1
    slot = lax.broadcasted_iota(jnp.int32, (1, 512), 1)
    row = jnp.where(slot < live, rows[...], 127)
    value = (slot + 1024 * block + 65536 * (row // 2)).astype(jnp.float32)
    lane = lax.broadcasted_iota(jnp.int32, (128, 128), 1)
    line = lax.broadcasted_iota(jnp.int32, (128, 128), 0)

    def down(x, g):
        return jnp.broadcast_to(x[:, 128 * g : 128 * g + 128], (128, 128)).T

    before = (lane < line).astype(jnp.bfloat16)
    row_f = row.astype(jnp.float32)
    members, ranks, total = [], [], jnp.zeros((1, 128), jnp.float32)
    for g in range(4):
        member = ((lane == down(row_f, g).astype(jnp.int32)) & (lane < 32)).astype(jnp.float32)
        rank = jnp.dot(before, member.astype(jnp.bfloat16), preferred_element_type=jnp.float32)
        ranks.append(rank + total)
        members.append(member)
        total = total + jnp.sum(member, axis=0, keepdims=True)
    groups = jnp.floor((total + 3.0) * 0.25)
    odd = lane % 2
    starts = 4.0 * jnp.dot(
        jnp.broadcast_to(groups, (8, 128)).astype(jnp.bfloat16),
        ((line < lane) & (line % 2 == odd)).astype(jnp.bfloat16),
        preferred_element_type=jnp.float32,
    )[:1]
    starts = starts + 640.0 * odd[:1].astype(jnp.float32)
    found = [jnp.zeros((1, 128), jnp.float32)] * 10
    for g in range(4):
        position = jnp.sum(members[g] * (ranks[g] + starts), axis=1, keepdims=True)
        alive = jnp.sum(members[g], axis=1, keepdims=True)
        position = jnp.where(alive > 0.0, position, -1.0).astype(jnp.int32)
        values = down(value, g)
        for t in range(10):
            hit = jnp.where(position == lane + 128 * t, values, 0.0)
            found[t] = found[t] + jnp.sum(hit, axis=0, keepdims=True)
    for t in range(10):
        plan[t : t + 1] = found[t].astype(jnp.int32)
    for half in range(2):
        mine = jnp.where(odd[:1] == half, groups, 0.0)
        quads = jnp.sum(mine, axis=1, keepdims=True).astype(jnp.int32)
        plan[10 + half : 11 + half] = jnp.broadcast_to(quads, (1, 128))
    plan[12:16] = jnp.zeros((4, 128), jnp.int32)


def make_plan(rows, columns, count, tiles):
    return pl.pallas_call(
        plan_kernel,
        out_shape=jax.ShapeDtypeStruct((16, 128), jnp.int32),
        in_specs=[pl.BlockSpec(memory_space=ANY)] * 2
        + [pl.BlockSpec(memory_space=SMEM), pl.BlockSpec(memory_space=VMEM)],
        out_specs=pl.BlockSpec(memory_space=VMEM),
        scratch_shapes=[
            VMEM((1, 512), jnp.int32),
            VMEM((1, 512), jnp.int32),
            pltpu.SemaphoreType.DMA((2,)),
        ],
        cost_estimate=pl.CostEstimate(flops=10**8, bytes_accessed=10**5, transcendentals=0),
        compiler_params=pltpu.CompilerParams(vmem_limit_bytes=8 * 2**20),
    )(in_hbm(rows), in_hbm(columns), count, resident(tiles))


def partial_gram(shards):
    total = None
    for s in range(4):
        x = shards[s]
        part = lax.dot_general(x, x, (((0,), (0,)), ((), ())), preferred_element_type=jnp.float32)
        total = part if total is None else total + part
    return total


def pack(shards):
    return pl.pallas_call(
        pack_only_kernel,
        out_shape=jax.ShapeDtypeStruct((4, 512, 128), jnp.bfloat16),
        in_specs=[pl.BlockSpec(memory_space=VMEM)] * 4,
        out_specs=pl.BlockSpec(memory_space=VMEM),
        compiler_params=pltpu.CompilerParams(vmem_limit_bytes=4 * 2**20),
    )(*shards)


def pack_only_kernel(own, first, second, third, near):
    for s, shard in enumerate((own, first, second, third)):
        near[s] = shard[...].T


def gram_kernel(shards, gram):
    gram[...] = partial_gram(shards)


def gram_of(shards):
    return pl.pallas_call(
        gram_kernel,
        out_shape=jax.ShapeDtypeStruct((128, 128), jnp.float32),
        in_specs=[pl.BlockSpec(memory_space=VMEM)],
        out_specs=pl.BlockSpec(memory_space=VMEM),
        compiler_params=pltpu.CompilerParams(vmem_limit_bytes=4 * 2**20),
    )(shards)


def products_kernel(half, plan_in, near, far, gram, tiles, *refs):
    outs, (sums, h_all, plan, plan_sem) = refs[:4], refs[4:]
    plan_copy = pltpu.make_async_copy(plan_in, plan, plan_sem)
    plan_copy.start()
    me, doc = lax.axis_index("term"), lax.axis_index("doc")
    my_x, my_z = doc // 4, lax.rem(doc, 4)
    sums[...] = jnp.zeros_like(sums)
    h_all[0] = jnp.zeros((128, 128), jnp.bfloat16)
    for s in range(4):
        for b in range(4):
            same = lax.rem(me + 8 - 2 * s, 8)
            other = same + 1 - 2 * lax.rem(me, 2)
            h_all[1 + same * 4 + b] = near[s, b * 128 : (b + 1) * 128, :]
            h_all[1 + other * 4 + b] = far[s, b * 128 : (b + 1) * 128, :]
    if half == 0:
        whole_gram = gram[...] + partial_gram(far)
    plan_copy.wait()

    @pl.loop(0, pl.cdiv(plan[10 + half, 0], UNROLL))
    def _(step):
        found, targets = [], []
        for u in range(UNROLL):
            first = (step * UNROLL + u) * 4
            left, right = [], []
            for i in range(4):
                entry = plan[5 * half + first // 128, first % 128 + i]
                left.append(tiles[entry & 1023])
                right.append(h_all[(entry >> 10) & 63])
                if i == 0:
                    to_x, to_z = entry >> 18, (entry >> 16) & 3
                    if half == 0:
                        targets.append(((to_x + 4 - my_x) & 3) * 4 + to_z)
                    else:
                        targets.append(((to_z + 4 - my_z) & 3) * 4 + to_x)
            found.append(
                jnp.dot(
                    jnp.concatenate(left, axis=1),
                    jnp.concatenate(right, axis=0),
                    preferred_element_type=jnp.float32,
                )
            )
        for u in range(UNROLL):
            sums[targets[u]] += found[u]

    for s in range(4):
        for b in range(4):
            outs[s][b * 128 : b * 128 + 128] = sums[4 * s + b]
        if half == 0:
            outs[s][512:640] = whole_gram


def tile_products(half, plan, near, far, gram, tiles):
    return pl.pallas_call(
        functools.partial(products_kernel, half),
        out_shape=[jax.ShapeDtypeStruct((640 if half == 0 else 512, 128), jnp.float32)] * 4,
        in_specs=[pl.BlockSpec(memory_space=ANY)] + [pl.BlockSpec(memory_space=VMEM)] * 4,
        out_specs=[pl.BlockSpec(memory_space=VMEM)] * 4,
        scratch_shapes=[
            VMEM((16, 128, 128), jnp.float32),
            VMEM((33, 128, 128), jnp.bfloat16),
            SMEM((16, 128), jnp.int32),
            pltpu.SemaphoreType.DMA,
        ],
        cost_estimate=pl.CostEstimate(flops=10**9, bytes_accessed=10**7, transcendentals=0),
        compiler_params=pltpu.CompilerParams(vmem_limit_bytes=8 * 2**20),
    )(plan, near, far, gram, resident(tiles))


def regroup_kernel(half, *refs):
    pieces, outs = refs[:4], refs[-4:]
    doc = lax.axis_index("doc")
    mine = lax.rem(doc, 4) if half == 0 else doc // 4
    for s in range(4):
        first = pl.multiple_of(((mine + s) & 3) * 128, 128)
        part = pl.ds(first, 128)
        outs[s][0:128] = (pieces[0][part] + pieces[1][part]) + (pieces[2][part] + pieces[3][part])
    if half == 0:
        gram = (pieces[0][512:] + pieces[1][512:]) + (pieces[2][512:] + pieces[3][512:])
        for s in range(4):
            outs[s][128:256] = gram


def regroup(half, pieces, after=()):
    return pl.pallas_call(
        functools.partial(regroup_kernel, half),
        out_shape=[jax.ShapeDtypeStruct((256 if half == 0 else 128, 128), jnp.float32)] * 4,
        in_specs=[pl.BlockSpec(memory_space=VMEM)] * 4
        + [pl.BlockSpec(memory_space=ANY)] * len(after),
        out_specs=[pl.BlockSpec(memory_space=VMEM)] * 4,
        compiler_params=pltpu.CompilerParams(vmem_limit_bytes=8 * 2**20),
    )(*pieces, *after)


def sweep_kernel(*refs):
    first, second, (w, fresh, squares) = refs[:4], refs[4:8], refs[8:]
    upper = (first[0][...] + first[1][...]) + (first[2][...] + first[3][...])
    lower = (second[0][...] + second[1][...]) + (second[2][...] + second[3][...])
    cross_t = jnp.concatenate([upper[:128].T, lower.T], axis=1)
    gram = upper[128:]
    row_id = lax.broadcasted_iota(jnp.int32, (128, 128), 0)
    col_id = lax.broadcasted_iota(jnp.int32, (128, 128), 1)
    diagonal = jnp.sum(jnp.where(row_id == col_id, gram, 0.0), axis=1, keepdims=True)
    inverse = 1.0 / diagonal
    w_t = w[...].T
    rest = cross_t - jnp.dot(
        gram, w_t, precision=lax.Precision.HIGHEST, preferred_element_type=jnp.float32
    )
    estimate = w_t + rest * inverse
    scaled = jnp.where(col_id < row_id, gram * inverse, 0.0)
    groups = [estimate[8 * q : 8 * q + 8] for q in range(16)]
    for k in range(128):
        q, s = divmod(k, 8)
        change = jnp.maximum(groups[q][s : s + 1], 0.0) - w_t[k : k + 1]
        for later in range(q, 16):
            groups[later] = groups[later] - scaled[8 * later : 8 * later + 8, k : k + 1] * change
    updated = jnp.maximum(jnp.concatenate(groups, axis=0), 0.0).T
    fresh[...] = updated
    squares[...] = jnp.broadcast_to(
        jnp.sum(updated * updated, axis=0, keepdims=True), (128, 128)
    )


def sweep(first, second, w):
    return pl.pallas_call(
        sweep_kernel,
        out_shape=(
            jax.ShapeDtypeStruct((256, 128), jnp.float32),
            jax.ShapeDtypeStruct((128, 128), jnp.float32),
        ),
        in_specs=[pl.BlockSpec(memory_space=VMEM)] * 9,
        out_specs=[pl.BlockSpec(memory_space=VMEM)] * 2,
        compiler_params=pltpu.CompilerParams(vmem_limit_bytes=16 * 2**20),
    )(*first, *second, w)


def scale_kernel(total_rows, squares, updated, out):
    total = jnp.sum(squares[...], axis=0, keepdims=True)
    rms = jnp.sqrt(total / total_rows + 1e-06)
    out[...] = updated[...] / rms


def scale(squares, updated, total_rows):
    return pl.pallas_call(
        functools.partial(scale_kernel, total_rows),
        out_shape=jax.ShapeDtypeStruct(updated.shape, jnp.float32),
    )(resident(squares), resident(updated))


def body(doc_tiles, tile_rows, tile_cols, tile_count, factor_h, factor_w):
    tiles = doc_tiles[0]
    own = factor_h
    shifted = [along_y(own, s) for s in (1, 2, 3)]
    plan = make_plan(tile_rows, tile_cols, tile_count, tiles)
    near, plan = lax.optimization_barrier((pack([own] + shifted), plan))
    far = other_core(near)

    gram = gram_of(near)
    even = tile_products(0, plan, near, far, gram, tiles)
    odd = tile_products(1, plan, near, far, gram, tiles)
    after = odd[0]
    even = [even[0]] + [along_x(even[s], s) for s in (1, 2, 3)]
    odd = [odd[0]] + [along_z(odd[s], s) for s in (1, 2, 3)]
    even = regroup(0, even, [after])
    even = [even[0]] + [along_z(even[s], s) for s in (1, 2, 3)]
    odd = regroup(1, odd)
    odd = [odd[0]] + [along_x(odd[s], s) for s in (1, 2, 3)]
    updated, squares = sweep(even, odd, factor_w)
    shared = lax.all_to_all(squares.reshape(128, 1, 128), ("term", "doc"), 0, 0)
    return scale(shared.reshape(128, 128), updated, 32768)


def solution(mesh):
    in_specs = (
        P("term", "doc", None, None),
        P("term", "doc"),
        P("term", "doc"),
        P("term", "doc"),
        P(None, ("term", "doc")),
        P(("term", "doc"), None),
    )
    out_specs = P(("term", "doc"), None)
    return jax.shard_map(body, mesh=mesh, in_specs=in_specs, out_specs=out_specs, check_vma=False)
```
